32 devices in a mesh: req: 8 (over y, x, core), head: 4 (over z).
Axes of the slice: x: 2, y: 2, z: 4, core: 2. Of those that a mesh axis runs over, the one named last changes fastest.
Arguments:
- prefill_query: bfloat16 [4096, 2048], P('req', 'head'), may hold values from -16 to 16
- prefill_new_pairs: bfloat16 [4096, 2, 1024], P('req', None, 'head'), may hold values from -16 to 16
- prefill_cache: bfloat16 [8, 2, 2048, 1024], P('req', None, None, 'head'), may hold values from -16 to 16
- prefill_start: int32 [8], P('req'), may hold values from 0 to 2048, as said below
- decode_query: bfloat16 [24, 2048], P('req', 'head'), may hold values from -16 to 16
- decode_fresh: bfloat16 [24, 2, 1024], P('req', None, 'head'), may hold values from -16 to 16
- decode_cache: bfloat16 [24, 2, 2048, 1024], P('req', None, None, 'head'), may hold values from -16 to 16
- decode_length: int32 [24], P('req'), may hold values from 2 to 2048
- decode_slot: int32 [24], P('req'), may hold values from 0 to 23, each once
- prefill_states: bfloat16 [4096, 2048], P('req', 'head'), may hold values from -32 to 32
- decode_states: bfloat16 [24, 2048], P('req', 'head'), may hold values from -32 to 32
- output_proj: bfloat16 [2048, 2048], P('head', 'req'), may hold values from -0.125 to 0.125
- norm_gain: bfloat16 [2048], replicated, may hold values from 0.099609375 to 1.8984375
- gate_weight: bfloat16 [2048, 6144], P('req', 'head'), may hold values from -0.125 to 0.125
- up_weight: bfloat16 [2048, 6144], P('req', 'head'), may hold values from -0.125 to 0.125
- down_weight: bfloat16 [6144, 2048], P('head', 'req'), may hold values from -0.078125 to 0.078125
Outputs:
- prefill_result: bfloat16 [4096, 2048], P('req', 'head')
- decode_result: bfloat16 [24, 2048], P('req', 'head')
The draws below stay inside these ranges and needn't reach their ends.
Inputs may be any that keep to these rules, and one draw needn't show every extreme that they name: `decode_slot`: a permutation; the cache of slot s is held by req index s // 3. `prefill_start`: a multiple of 512.
All inputs are finite; a program needn't handle non-finite values.
Results may differ from the reference program's by a relative error of at most 0.0094.
Values may be sent and summed in bfloat16 or wider, within the bound.
A program may use at most 128 MiB of HBM per device.

```python
import math
import jax
import jax.numpy as jnp
from jax import lax

D = 2048
HQ = 16
KEY_VALUE_HEADS = 8
HEAD_SIZE = 128
FF = 6144
REQUEST_TOKENS = 512
CACHE_POSITIONS = 2048
PREFILL_REQUESTS = 8
DECODE_REQUESTS = 24
PREFILL_TOKENS = 4096


def normal_base(key, target_dims):
    return jax.random.truncated_normal(key, -4.0, 4.0, target_dims, jnp.float32)


def draw_prefill_query(key, part):
    target_dims = (PREFILL_TOKENS, HQ, HEAD_SIZE)
    base_draw = normal_base(key, target_dims)
    return base_draw.reshape(PREFILL_TOKENS, HQ * HEAD_SIZE).astype(jnp.bfloat16)


def draw_decode_query(key, part):
    target_dims = (DECODE_REQUESTS, HQ, HEAD_SIZE)
    base_draw = normal_base(key, target_dims)
    return base_draw.reshape(DECODE_REQUESTS, HQ * HEAD_SIZE).astype(jnp.bfloat16)


def draw_prefill_new_pairs(key, part):
    target_dims = (PREFILL_TOKENS, KEY_VALUE_HEADS, HEAD_SIZE)
    key_part = normal_base(jax.random.fold_in(key, 1), target_dims)
    value_part = 4.0 * normal_base(jax.random.fold_in(key, 2), target_dims)
    combined_rows = jnp.stack([key_part, value_part], axis=1)
    return combined_rows.reshape(PREFILL_TOKENS, 2, KEY_VALUE_HEADS * HEAD_SIZE).astype(jnp.bfloat16)


def draw_decode_fresh(key, part):
    target_dims = (DECODE_REQUESTS, KEY_VALUE_HEADS, HEAD_SIZE)
    key_part = normal_base(jax.random.fold_in(key, 1), target_dims)
    value_part = 4.0 * normal_base(jax.random.fold_in(key, 2), target_dims)
    combined_rows = jnp.stack([key_part, value_part], axis=1)
    return combined_rows.reshape(DECODE_REQUESTS, 2, KEY_VALUE_HEADS * HEAD_SIZE).astype(jnp.bfloat16)


def cache_draw(key, request_count_all):
    target_dims = (request_count_all, CACHE_POSITIONS, KEY_VALUE_HEADS, HEAD_SIZE)
    key_part = normal_base(jax.random.fold_in(key, 1), target_dims)
    value_part = 4.0 * normal_base(jax.random.fold_in(key, 2), target_dims)
    combined_rows = jnp.stack([key_part, value_part], axis=1)
    return combined_rows.reshape(request_count_all, 2, CACHE_POSITIONS, KEY_VALUE_HEADS * HEAD_SIZE).astype(jnp.bfloat16)


def draw_prefill_cache(key, part):
    return cache_draw(key, PREFILL_REQUESTS)


def draw_decode_cache(key, part):
    return cache_draw(key, DECODE_REQUESTS)


def draw_decode_length(key, part):
    lengths = jax.random.randint(key, (DECODE_REQUESTS,), 2, CACHE_POSITIONS + 1, dtype=jnp.int32)
    longest = jax.random.randint(jax.random.fold_in(key, 1), (), 0, DECODE_REQUESTS, dtype=jnp.int32)
    return jnp.where(jnp.arange(DECODE_REQUESTS, dtype=jnp.int32) == longest, CACHE_POSITIONS, lengths).astype(jnp.int32)


def draw_prefill_start(key, part):
    step_count = jax.random.randint(key, (PREFILL_REQUESTS,), 0, CACHE_POSITIONS // REQUEST_TOKENS + 1, dtype=jnp.int32)
    longest = jax.random.randint(jax.random.fold_in(key, 1), (), 0, PREFILL_REQUESTS, dtype=jnp.int32)
    step_count = jnp.where(jnp.arange(PREFILL_REQUESTS, dtype=jnp.int32) == longest, CACHE_POSITIONS // REQUEST_TOKENS, step_count)
    return (step_count * REQUEST_TOKENS).astype(jnp.int32)


def states_draw(key, row_total):
    ramp = jnp.power(3.0, jnp.arange(D, dtype=jnp.float32) / D - 0.5)
    base_draw = normal_base(jax.random.fold_in(key, 1), (row_total, D))
    row_scale = jnp.exp(jax.random.uniform(jax.random.fold_in(key, 2), (row_total, 1), jnp.float32, -1.2, 1.2))
    return (base_draw * row_scale * ramp[None, :]).astype(jnp.bfloat16)


def draw_prefill_states(key, part):
    return states_draw(key, PREFILL_TOKENS)


def draw_decode_states(key, part):
    return states_draw(key, DECODE_REQUESTS)


def levels(rng, shape, shards, low, top_value):
    factor_of = 1.0
    for axis_at, blocks in shards:
        steps = jax.random.uniform(jax.random.fold_in(jax.random.fold_in(rng, 6), axis_at), (blocks,), jnp.float32, low / len(shards), top_value / len(shards))
        factor_of = factor_of * jnp.repeat(jnp.exp(steps), shape[axis_at] // blocks).reshape((-1,) + (1,) * (len(shape) - 1 - axis_at))
    return factor_of


def centred(own_key, shape, deviation, most, pieces=(), kind=jnp.bfloat16):
    values = jax.random.normal(own_key, shape, jnp.float32) * deviation
    if len(pieces) > 0:
        values = levels(own_key, shape, pieces, -0.22, 0.18) * values
    return jnp.clip(values, min=-most, max=most).astype(kind)


def setup_inputs(seed: int = 0) -> dict:
    keys = jax.random.split(jax.random.key(seed), 17)
    prefill_query = draw_prefill_query(jax.random.fold_in(keys[16], 71), 0)
    prefill_new_pairs = draw_prefill_new_pairs(jax.random.fold_in(keys[16], 71), 0)
    prefill_cache = draw_prefill_cache(jax.random.fold_in(keys[16], 71), 0)
    prefill_start = draw_prefill_start(jax.random.fold_in(keys[16], 71), 0)
    decode_query = draw_decode_query(jax.random.fold_in(keys[16], 71), 0)
    decode_fresh = draw_decode_fresh(jax.random.fold_in(keys[16], 71), 0)
    decode_cache = draw_decode_cache(jax.random.fold_in(keys[16], 71), 0)
    decode_length = draw_decode_length(jax.random.fold_in(keys[16], 71), 0)
    decode_slot = jax.random.permutation(keys[8], DECODE_REQUESTS).astype(jnp.int32)
    prefill_states = draw_prefill_states(jax.random.fold_in(keys[16], 71), 0)
    decode_states = draw_decode_states(jax.random.fold_in(keys[16], 71), 0)
    output_proj = centred(keys[11], (HQ * HEAD_SIZE, D), (HQ * HEAD_SIZE) ** -0.5, 0.125, ((0, 4), (1, 8)))
    norm_gain = jnp.clip(1.0 + 0.18 * jax.random.normal(keys[12], (D,), jnp.float32), 0.099609375, 1.8984375).astype(jnp.bfloat16)
    gate_weight = centred(keys[13], (D, FF), D ** -0.5, 0.125, ((0, 8), (1, 4)))
    up_weight = centred(keys[14], (D, FF), D ** -0.5, 0.125, ((0, 8), (1, 4)))
    down_weight = centred(keys[15], (FF, D), FF ** -0.5, 0.078125, ((0, 4), (1, 8)))
    return {"prefill_query": prefill_query, "prefill_new_pairs": prefill_new_pairs, "prefill_cache": prefill_cache, "prefill_start": prefill_start, "decode_query": decode_query, "decode_fresh": decode_fresh, "decode_cache": decode_cache, "decode_length": decode_length, "decode_slot": decode_slot, "prefill_states": prefill_states, "decode_states": decode_states, "output_proj": output_proj, "norm_gain": norm_gain, "gate_weight": gate_weight, "up_weight": up_weight, "down_weight": down_weight}


rope_base = 1000000.0
norm_eps = 1e-06

def rope_tables(positions, head_size):
    half_size = head_size // 2
    lane_index = jnp.arange(half_size, dtype=jnp.float32)
    inverse = jnp.power(jnp.float32(rope_base), -2.0 * lane_index / head_size)
    angles = positions.astype(jnp.float32)[:, None] * inverse[None, :]
    cosine = jnp.concatenate([jnp.cos(angles), jnp.cos(angles)], axis=1)
    sine_table = jnp.concatenate([jnp.sin(angles), jnp.sin(angles)], axis=1)
    return (cosine, sine_table)

def rotate(vectors, cosine, sine_table):
    half_size = vectors.shape[-1] // 2
    front_half = vectors[..., :half_size]
    back_half = vectors[..., half_size:]
    turned = jnp.concatenate([-back_half, front_half], axis=-1)
    return vectors * cosine[:, None, :] + turned * sine_table[:, None, :]

def attend(query_rows, key_rows, value_rows, visible):
    row_count, head_count, head_size = query_rows.shape
    groups = key_rows.shape[1]
    grouped = query_rows.reshape(row_count, groups, head_count // groups, head_size).astype(jnp.float32)
    scores = jnp.einsum('qhgd,khd->hgqk', grouped, key_rows.astype(jnp.float32)) * (1.0 / math.sqrt(head_size))
    scores = jnp.where(visible[None, None], scores, -jnp.inf)
    highest = lax.optimization_barrier(jnp.max(scores, axis=-1, keepdims=True))
    unnormed = jnp.exp(scores - highest)
    totals = lax.optimization_barrier(jnp.sum(unnormed, axis=-1, keepdims=True))
    rounded = unnormed.astype(jnp.bfloat16)
    blended = jnp.einsum('hgqk,khd->qhgd', rounded.astype(jnp.float32), value_rows.astype(jnp.float32))
    blended = blended / jnp.transpose(totals, (2, 0, 1, 3))
    return blended.reshape(row_count, head_count * head_size).astype(jnp.bfloat16)

def prefill_task(query_rows, fresh_rows, cache_rows, offset_value, head_size):
    span_len = query_rows.shape[0]
    positions = offset_value + jnp.arange(span_len, dtype=jnp.int32)
    cosine, sine_table = rope_tables(positions, head_size)
    head_count = query_rows.shape[1] // head_size
    groups = fresh_rows.shape[2] // head_size
    rot_query = rotate(query_rows.astype(jnp.float32).reshape(span_len, head_count, head_size), cosine, sine_table).astype(jnp.bfloat16)
    rot_key = rotate(fresh_rows[:, 0].astype(jnp.float32).reshape(span_len, groups, head_size), cosine, sine_table).astype(jnp.bfloat16)
    cache_len = cache_rows.shape[1]
    key_rows = jnp.concatenate([cache_rows[0].reshape(cache_len, groups, head_size), rot_key], axis=0)
    value_rows = jnp.concatenate([cache_rows[1].reshape(cache_len, groups, head_size), fresh_rows[:, 1].reshape(span_len, groups, head_size)], axis=0)
    cache_seen = jnp.broadcast_to(jnp.arange(cache_len, dtype=jnp.int32)[None, :] < offset_value, (span_len, cache_len))
    own_seen = jnp.arange(span_len, dtype=jnp.int32)[None, :] <= jnp.arange(span_len, dtype=jnp.int32)[:, None]
    visible = jnp.concatenate([cache_seen, own_seen], axis=1)
    return attend(rot_query, key_rows, value_rows, visible)

def decode_task(query_rows, fresh_rows, cache_rows, length, head_size):
    positions = jnp.reshape(length, (1,)).astype(jnp.int32)
    cosine, sine_table = rope_tables(positions, head_size)
    head_count = query_rows.shape[0] // head_size
    groups = fresh_rows.shape[1] // head_size
    rot_query = rotate(query_rows.astype(jnp.float32).reshape(1, head_count, head_size), cosine, sine_table).astype(jnp.bfloat16)
    rot_key = rotate(fresh_rows[0].astype(jnp.float32).reshape(1, groups, head_size), cosine, sine_table).astype(jnp.bfloat16)
    cache_len = cache_rows.shape[1]
    key_rows = jnp.concatenate([cache_rows[0].reshape(cache_len, groups, head_size), rot_key], axis=0)
    value_rows = jnp.concatenate([cache_rows[1].reshape(cache_len, groups, head_size), fresh_rows[1].reshape(1, groups, head_size)], axis=0)
    visible = jnp.concatenate([jnp.arange(cache_len, dtype=jnp.int32)[None, :] < length, jnp.ones((1, 1), jnp.bool_)], axis=1)
    return attend(rot_query, key_rows, value_rows, visible)[0]

def reference(prefill_query, prefill_new_pairs, prefill_cache, prefill_start, decode_query, decode_fresh, decode_cache, decode_length, decode_slot, prefill_states, decode_states, output_proj, norm_gain, gate_weight, up_weight, down_weight):
    query_blocks = prefill_query.reshape(PREFILL_REQUESTS, REQUEST_TOKENS, HQ * HEAD_SIZE)
    newest_blocks = prefill_new_pairs.reshape(PREFILL_REQUESTS, REQUEST_TOKENS, 2, KEY_VALUE_HEADS * HEAD_SIZE)
    prefill_att = lax.map(lambda operands: prefill_task(operands[0], operands[1], operands[2], operands[3], HEAD_SIZE), (query_blocks, newest_blocks, prefill_cache, prefill_start))
    prefill_att = prefill_att.reshape(PREFILL_TOKENS, HQ * HEAD_SIZE)
    slot_query = jnp.zeros_like(decode_query).at[decode_slot].set(decode_query)
    slot_fresh = jnp.zeros_like(decode_fresh).at[decode_slot].set(decode_fresh)
    slot_att = lax.map(lambda operands: decode_task(operands[0], operands[1], operands[2], operands[3], HEAD_SIZE), (slot_query, slot_fresh, decode_cache, decode_length))
    decode_att = slot_att[decode_slot]
    attended = jnp.concatenate([prefill_att, decode_att], axis=0)
    states = jnp.concatenate([prefill_states, decode_states], axis=0)
    summed = states.astype(jnp.float32) + jnp.dot(attended, output_proj, preferred_element_type=jnp.float32)
    mean_square = lax.optimization_barrier(jnp.mean(summed * summed, axis=1, keepdims=True))
    normed = (summed * lax.rsqrt(mean_square + norm_eps) * norm_gain.astype(jnp.float32)).astype(jnp.bfloat16)
    gate_sum = jnp.dot(normed, gate_weight, preferred_element_type=jnp.float32)
    upper = jnp.dot(normed, up_weight, preferred_element_type=jnp.float32)
    hidden = (jax.nn.silu(gate_sum) * upper).astype(jnp.bfloat16)
    result = (summed + jnp.dot(hidden, down_weight, preferred_element_type=jnp.float32)).astype(jnp.bfloat16)
    return (result[:PREFILL_TOKENS], result[PREFILL_TOKENS:])
```

```python
import functools
import math

import jax
import jax.numpy as jnp
from jax import lax
from jax.experimental import pallas as pl
from jax.experimental.pallas import tpu as pltpu
from jax.sharding import PartitionSpec as P

HEAD_SIZE = 128
REQUEST_TOKENS = 512


rope_base = 1000000.0
norm_eps = 1e-06


def rope_tables(positions, head_size):
    half_size = head_size // 2
    lane_index = jnp.arange(half_size, dtype=jnp.float32)
    inverse = jnp.power(jnp.float32(rope_base), -2.0 * lane_index / head_size)
    angles = positions.astype(jnp.float32)[:, None] * inverse[None, :]
    cosine = jnp.concatenate([jnp.cos(angles), jnp.cos(angles)], axis=1)
    sine_table = jnp.concatenate([jnp.sin(angles), jnp.sin(angles)], axis=1)
    return (cosine, sine_table)


def rotate(vectors, cosine, sine_table):
    half_size = vectors.shape[-1] // 2
    front_half = vectors[..., :half_size]
    back_half = vectors[..., half_size:]
    turned = jnp.concatenate([-back_half, front_half], axis=-1)
    return vectors * cosine[:, None, :] + turned * sine_table[:, None, :]


def attend(query_rows, key_rows, value_rows, visible):
    row_count, head_count, head_size = query_rows.shape
    groups = key_rows.shape[1]
    grouped = query_rows.reshape(row_count, groups, head_count // groups, head_size)
    scores = jnp.einsum("qhgd,khd->hgqk", grouped, key_rows, preferred_element_type=jnp.float32) * (
        1.0 / math.sqrt(head_size)
    )
    scores = jnp.where(visible[None, None], scores, -jnp.inf)
    highest = jnp.max(scores, axis=-1, keepdims=True)
    unnormed = jnp.exp(scores - highest)
    totals = jnp.sum(unnormed, axis=-1, keepdims=True)
    rounded = unnormed.astype(jnp.bfloat16)
    blended = jnp.einsum("hgqk,khd->qhgd", rounded, value_rows, preferred_element_type=jnp.float32)
    blended = blended / jnp.transpose(totals, (2, 0, 1, 3))
    return blended.reshape(row_count, head_count * head_size).astype(jnp.bfloat16)


def prefill_task(query_rows, fresh_rows, cache_rows, offset_value, head_size):
    span_len = query_rows.shape[0]
    positions = offset_value + jnp.arange(span_len, dtype=jnp.int32)
    cosine, sine_table = rope_tables(positions, head_size)
    head_count = query_rows.shape[1] // head_size
    groups = fresh_rows.shape[2] // head_size
    rot_query = rotate(
        query_rows.astype(jnp.float32).reshape(span_len, head_count, head_size), cosine, sine_table
    ).astype(jnp.bfloat16)
    rot_key = rotate(
        fresh_rows[:, 0].astype(jnp.float32).reshape(span_len, groups, head_size),
        cosine,
        sine_table,
    ).astype(jnp.bfloat16)
    cache_len = cache_rows.shape[1]
    key_rows = jnp.concatenate(
        [cache_rows[0].reshape(cache_len, groups, head_size), rot_key], axis=0
    )
    value_rows = jnp.concatenate(
        [
            cache_rows[1].reshape(cache_len, groups, head_size),
            fresh_rows[:, 1].reshape(span_len, groups, head_size),
        ],
        axis=0,
    )
    cache_seen = jnp.broadcast_to(
        jnp.arange(cache_len, dtype=jnp.int32)[None, :] < offset_value, (span_len, cache_len)
    )
    own_seen = (
        jnp.arange(span_len, dtype=jnp.int32)[None, :]
        <= jnp.arange(span_len, dtype=jnp.int32)[:, None]
    )
    visible = jnp.concatenate([cache_seen, own_seen], axis=1)
    return attend(rot_query, key_rows, value_rows, visible)


def decode_task(query_rows, fresh_rows, cache_rows, length, head_size):
    positions = jnp.reshape(length, (1,))
    cosine, sine_table = rope_tables(positions, head_size)
    head_count = query_rows.shape[0] // head_size
    groups = fresh_rows.shape[1] // head_size
    rot_query = rotate(
        query_rows.astype(jnp.float32).reshape(1, head_count, head_size), cosine, sine_table
    ).astype(jnp.bfloat16)
    rot_key = rotate(
        fresh_rows[0].astype(jnp.float32).reshape(1, groups, head_size), cosine, sine_table
    ).astype(jnp.bfloat16)
    cache_len = cache_rows.shape[1]
    key_rows = jnp.concatenate(
        [cache_rows[0].reshape(cache_len, groups, head_size), rot_key], axis=0
    )
    value_rows = jnp.concatenate(
        [
            cache_rows[1].reshape(cache_len, groups, head_size),
            fresh_rows[1].reshape(1, groups, head_size),
        ],
        axis=0,
    )
    visible = jnp.concatenate(
        [jnp.arange(cache_len, dtype=jnp.int32)[None, :] < length, jnp.ones((1, 1), jnp.bool_)],
        axis=1,
    )
    return attend(rot_query, key_rows, value_rows, visible)[0]


def decode_attend(own_query, own_fresh, decode_cache, decode_length):

    def one_slot(query_rows, fresh_rows, cache_rows, length):
        return decode_task(query_rows, fresh_rows, cache_rows, length, HEAD_SIZE)

    return jax.vmap(one_slot)(own_query, own_fresh, decode_cache, decode_length)


def body(
    prefill_query,
    prefill_new_pairs,
    prefill_cache,
    prefill_start,
    decode_query,
    decode_fresh,
    decode_cache,
    decode_length,
    decode_slot,
    prefill_states,
    decode_states,
    output_proj,
    norm_gain,
    gate_weight,
    up_weight,
    down_weight,
):
    local_prefills = prefill_query.shape[0] // REQUEST_TOKENS
    query_blocks = prefill_query.reshape(local_prefills, REQUEST_TOKENS, prefill_query.shape[1])
    newest_blocks = prefill_new_pairs.reshape(
        local_prefills, REQUEST_TOKENS, 2, prefill_new_pairs.shape[2]
    )
    prefill_att = lax.map(
        lambda operands: prefill_task(
            operands[0], operands[1], operands[2], operands[3], HEAD_SIZE
        ),
        (query_blocks, newest_blocks, prefill_cache, prefill_start),
    )
    prefill_att = prefill_att.reshape(local_prefills * REQUEST_TOKENS, prefill_query.shape[1])
    local_decodes = decode_query.shape[0]
    fresh_width = decode_fresh.shape[2]
    fresh_flat = decode_fresh.reshape(local_decodes, 2 * fresh_width)
    slot_marks = decode_slot.astype(jnp.bfloat16)
    every_query, every_fresh, every_slot = (
        lax.all_gather(decode_query, "req", axis=0, tiled=True),
        lax.all_gather(fresh_flat, "req", axis=0, tiled=True),
        lax.all_gather(slot_marks, "req", axis=0, tiled=True),
    )
    owned = lax.axis_index("req") * local_decodes + jnp.arange(local_decodes, dtype=jnp.int32)
    picker = (every_slot.astype(jnp.int32)[None, :] == owned[:, None]).astype(jnp.bfloat16)
    own_query = jnp.dot(picker, every_query, preferred_element_type=jnp.float32).astype(
        jnp.bfloat16
    )
    own_fresh = jnp.dot(picker, every_fresh, preferred_element_type=jnp.float32).astype(
        jnp.bfloat16
    )
    own_att = decode_attend(
        own_query, own_fresh.reshape(local_decodes, 2, fresh_width), decode_cache, decode_length
    )
    every_att = lax.all_gather(own_att, "req", axis=0, tiled=True)
    total_slots = every_att.shape[0]
    chooser = (decode_slot[:, None] == jnp.arange(total_slots, dtype=jnp.int32)[None, :]).astype(
        jnp.bfloat16
    )
    decode_att = jnp.dot(chooser, every_att, preferred_element_type=jnp.float32).astype(
        jnp.bfloat16
    )
    attended = jnp.concatenate([prefill_att, decode_att], axis=0)
    states = jnp.concatenate([prefill_states, decode_states], axis=0)
    partial_value = jnp.dot(
        attended,
        lax.all_gather(output_proj, "req", axis=1, tiled=True),
        preferred_element_type=jnp.float32,
    )
    model_width = partial_value.shape[1]
    share_cols = model_width // lax.axis_size("head")
    share_start = lax.axis_index("head") * share_cols
    summed = lax.psum_scatter(
        partial_value, "head", scatter_dimension=1, tiled=True
    ) + states.astype(jnp.float32)
    squares = lax.psum(jnp.sum(summed * summed, axis=1), "head")
    gain_share = lax.dynamic_slice_in_dim(norm_gain, share_start, share_cols, 0).astype(jnp.float32)
    normed_share = (
        summed * lax.rsqrt(squares[:, None] / model_width + norm_eps) * gain_share
    ).astype(jnp.bfloat16)
    normed = lax.all_gather(normed_share, "head", axis=1, tiled=True)

    def add_rows(weight_piece):
        return jnp.dot(normed, weight_piece, preferred_element_type=jnp.float32)

    gate_sum = add_rows(lax.all_gather(gate_weight, "req", axis=0, tiled=True))
    upper = add_rows(lax.all_gather(up_weight, "req", axis=0, tiled=True))
    hidden = (jax.nn.silu(gate_sum) * upper).astype(jnp.bfloat16)
    down_terms = jnp.dot(
        hidden,
        lax.all_gather(down_weight, "req", axis=1, tiled=True),
        preferred_element_type=jnp.float32,
    )
    result = (
        summed + lax.psum_scatter(down_terms, "head", scatter_dimension=1, tiled=True)
    ).astype(jnp.bfloat16)
    prefill_rows = prefill_att.shape[0]
    return (result[:prefill_rows], result[prefill_rows:])


MESH = pl.DeviceIdType.MESH
BF = jnp.bfloat16
F32 = jnp.float32
CHUNKS = 3
PAD = 16


def mm(a, b):
    return jnp.dot(a, b, preferred_element_type=F32)


def mm_t(a, b):
    return lax.dot_general(a, b, (((1,), (1,)), ((), ())), preferred_element_type=F32)


def turn(x, cosine, signed_sine):
    return x * cosine + pltpu.roll(x, 64, 1) * signed_sine


class Gather:
    def __init__(self, me, shard, slot_of, send, recv, own):
        self.me = me
        self.sib = me + 1 - 2 * (me % 2)
        self.xn = me + 2 - 4 * ((me // 2) % 2)
        self.yn = me + 4 - 8 * (me // 4)
        self.dg = self.yn + 2 - 4 * ((me // 2) % 2)
        self.half = shard.shape[0] // 2
        self.shard, self.slot, self.send, self.recv, self.own = shard, slot_of, send, recv, own

    def copy(self, at, src, dst, to):
        return pltpu.make_async_remote_copy(
            src_ref=src,
            dst_ref=dst,
            send_sem=self.send.at[at],
            recv_sem=self.recv.at[at],
            device_id={"req": to},
            device_id_type=MESH,
        )

    def part(self, who, k):
        return self.slot(who).at[pl.ds(k * self.half, self.half)]

    def copies(self):
        mine = self.slot(self.me)
        sx, sy = self.slot(self.xn), self.slot(self.yn)
        d0, d1 = self.part(self.dg, 0), self.part(self.dg, 1)
        x0, y1 = self.part(self.xn, 0), self.part(self.yn, 1)
        return [
            self.copy(0, self.shard, mine, self.xn),
            self.copy(1, self.shard, mine, self.yn),
            self.copy(2, self.shard, mine, self.sib),
            self.copy(3, x0, x0, self.yn),
            self.copy(4, sx, sx, self.sib),
            self.copy(5, y1, y1, self.xn),
            self.copy(6, sy, sy, self.sib),
            self.copy(7, d0, d0, self.sib),
            self.copy(8, d1, d1, self.sib),
        ]

    def begin(self):
        self.all = self.copies()
        for at in (0, 1, 2):
            self.all[at].start()
        self.local = pltpu.make_async_copy(self.shard, self.slot(self.me), self.own)
        self.local.start()

    def middle(self):
        self.all[0].wait_recv()
        self.all[3].start()
        self.all[4].start()
        self.all[1].wait_recv()
        self.all[5].start()
        self.all[6].start()

    def last(self):
        self.all[3].wait_recv()
        self.all[7].start()
        self.all[5].wait_recv()
        self.all[8].start()

    def finish(self):
        for at in (2, 4, 6, 7, 8):
            self.all[at].wait_recv()
        for one in self.all:
            one.wait_send()
        self.local.wait()


def attention_kernel(
    n, slots,
    q_ref, fk_ref, fv_ref, pc_ref, cos_ref, sin_ref, start_ref,
    tok_ref, dcos_ref, dsin_ref, dlen_ref, rid_ref, dc_ref, proj_ref, gate_ref,
    att_ref, projg_ref, gateg_ref,
    kbuf, vbuf, dbuf, toks, atts, myatt, qrot,
    local_sem, tok_send, tok_recv, att_send, att_recv, w_send, w_recv,
):
    me = lax.axis_index("req")
    cache = pc_ref.shape[1]
    span = q_ref.shape[0]
    loads = [
        pltpu.make_async_copy(dc_ref, dbuf, local_sem.at[0]),
        pltpu.make_async_copy(pc_ref.at[0], kbuf.at[pl.ds(0, cache)], local_sem.at[1]),
        pltpu.make_async_copy(pc_ref.at[1], vbuf.at[pl.ds(0, cache)], local_sem.at[2]),
    ]
    for one in loads:
        one.start()
    barrier = pltpu.get_barrier_semaphore()
    for j in range(1, n):
        pl.semaphore_signal(
            barrier, inc=1, device_id={"req": (me + j) % n}, device_id_type=MESH
        )
    pl.semaphore_wait(barrier, n - 1)

    def spread(src, dst, send, recv):
        return [
            pltpu.make_async_remote_copy(
                src_ref=src,
                dst_ref=dst.at[me],
                send_sem=send.at[j],
                recv_sem=recv.at[j],
                device_id={"req": (me + j) % n},
                device_id_type=MESH,
            )
            for j in range(1, n)
        ]

    tok_copies = spread(tok_ref, toks, tok_send, tok_recv)
    for one in tok_copies:
        one.start()
    rows_of = gate_ref.shape[0]
    first = Gather(
        me, proj_ref, lambda who: projg_ref.at[who], w_send.at[0], w_recv.at[0], local_sem.at[3]
    )
    second = Gather(
        me, gate_ref, lambda who: gateg_ref.at[pl.ds(who * rows_of, rows_of)],
        w_send.at[1], w_recv.at[1], local_sem.at[4],
    )
    first.begin()
    second.begin()
    toks[me] = tok_ref[...]

    factor = 1.4426950408889634 / math.sqrt(HEAD_SIZE)
    for h in range(4):
        at = pl.ds(h * 128, 128)
        qrot[:, at] = turn(q_ref[:, at].astype(F32), cos_ref[...], sin_ref[...]).astype(BF)
    for one in loads:
        one.wait()
    for g in range(2):
        at = pl.ds(g * 128, 128)
        kbuf[pl.ds(cache, span), at] = turn(
            fk_ref[:, at].astype(F32), cos_ref[...], sin_ref[...]
        ).astype(BF)
    vbuf[pl.ds(cache, span), :] = fv_ref[...]

    for one in tok_copies:
        one.wait_recv()
    tokens = toks[...].reshape(n * PAD, toks.shape[2])
    marks = tokens[:, 1024:1152].astype(F32)
    lane = lax.broadcasted_iota(jnp.int32, marks.shape, 1)
    wanted = jnp.where(lane < slots, me * slots + lane, -7).astype(F32)
    picker = jnp.where(marks == wanted, 1.0, 0.0).T[:PAD].astype(BF)
    own = mm(picker, tokens[:, :1024])[:8]
    dcos, dsin = dcos_ref[...], dsin_ref[...]
    row16 = lax.broadcasted_iota(jnp.int32, (16, 1), 0) % 8
    col = lax.broadcasted_iota(jnp.int32, (16, cache), 1)
    seen = col < dlen_ref[:, 0:1]
    for g in range(2):
        heads = [
            turn(own[:, (2 * g + j) * 128:(2 * g + j + 1) * 128], dcos, dsin) for j in range(2)
        ]
        query = jnp.concatenate(heads, axis=0).astype(BF)
        key = turn(own[:, 512 + g * 128:512 + (g + 1) * 128], dcos, dsin).astype(BF).astype(F32)
        value = own[:, 768 + g * 128:768 + (g + 1) * 128]
        at = pl.ds(g * 128, 128)
        scores = jnp.zeros((16, cache), F32)
        for s in range(slots):
            scores = jnp.where(row16 == s, mm_t(query, dbuf[s, 0, :, at]), scores)
        scores = jnp.where(seen, scores, -1e30)
        new = jnp.sum(
            query.astype(F32) * jnp.concatenate([key, key], axis=0), axis=1, keepdims=True
        )
        top = jnp.maximum(jnp.max(scores, axis=1, keepdims=True), new)
        raw = jnp.exp2((scores - top) * factor)
        raw_new = jnp.exp2((new - top) * factor)
        totals = jnp.sum(raw, axis=1, keepdims=True) + raw_new
        raw16 = raw.astype(BF)
        mixed = jnp.zeros((16, 128), F32)
        for s in range(slots):
            mixed = jnp.where(row16 == s, mm(raw16, dbuf[s, 1, :, at]), mixed)
        mixed = mixed + raw_new.astype(BF).astype(F32) * jnp.concatenate([value, value], axis=0)
        mixed = mixed / totals
        for j in range(2):
            piece = jnp.concatenate([mixed[j * 8:j * 8 + 8], jnp.zeros((8, 128), F32)], axis=0)
            myatt[:, pl.ds((2 * g + j) * 128, 128)] = piece.astype(BF)
    att_copies = spread(myatt, atts, att_send, att_recv)
    for one in att_copies:
        one.start()
    atts[me] = myatt[...]
    first.middle()

    start = start_ref[0:1, 0:1]
    bias = jnp.where(lax.broadcasted_iota(jnp.int32, (1, cache), 1) < start, 0.0, -1e30)
    block = 128
    for g in range(2):
        at = pl.ds(g * 128, 128)

        def one_block(i, carry, g=g, at=at):
            rows = pl.ds(pl.multiple_of(i * block, block), block)
            query = jnp.concatenate(
                [qrot[rows, pl.ds((2 * g + j) * 128, 128)] for j in range(2)], axis=0
            )
            old = mm_t(query, kbuf[pl.ds(0, cache), at]) + bias
            new = mm_t(query, kbuf[pl.ds(cache, span), at])
            row = lax.broadcasted_iota(jnp.int32, new.shape, 0) % block + i * block
            new = jnp.where(lax.broadcasted_iota(jnp.int32, new.shape, 1) <= row, new, -1e30)
            top = jnp.maximum(
                jnp.max(old, axis=1, keepdims=True), jnp.max(new, axis=1, keepdims=True)
            )
            raw_old = jnp.exp2((old - top) * factor)
            raw_new = jnp.exp2((new - top) * factor)
            totals = jnp.sum(raw_old, axis=1, keepdims=True) + jnp.sum(
                raw_new, axis=1, keepdims=True
            )
            mixed = mm(raw_old.astype(BF), vbuf[pl.ds(0, cache), at]) + mm(
                raw_new.astype(BF), vbuf[pl.ds(cache, span), at]
            )
            mixed = (mixed / totals).astype(BF)
            for j in range(2):
                att_ref[rows, pl.ds((2 * g + j) * 128, 128)] = mixed[j * block:(j + 1) * block]
            return carry

        lax.fori_loop(0, span // block, one_block, 0)
        if g == 0:
            second.middle()
            first.last()
    for one in att_copies:
        one.wait_recv()
    every = atts[...].reshape(n * PAD, atts.shape[2])
    pick = lax.broadcasted_iota(jnp.int32, (PAD, n * PAD), 1) == rid_ref[:, 0:1]
    att_ref[pl.ds(span, PAD), :] = mm(jnp.where(pick, 1.0, 0.0).astype(BF), every).astype(BF)
    second.last()
    first.finish()
    second.finish()
    for one in tok_copies + att_copies:
        one.wait_send()


def layer_kernel(
    heads,
    att_ref, st_ref, projg_ref, gain_ref, gateg_ref, up_ref, down_ref,
    res_ref,
    terms, summed, gath, hidden, gate_v, up_v, down_v,
    up1, dn1, up1s, dn1s, up2, dn2, up2s, dn2s,
    local_sem, w_send, w_recv, rs_send, rs_recv, ag_send, ag_recv,
):
    me = lax.axis_index("req")
    z = lax.axis_index("head")
    top = heads - 1
    rows = gath.shape[2]
    share = gath.shape[3]
    width = heads * share
    rows_of = up_ref.shape[0]
    gate_load = pltpu.make_async_copy(gateg_ref, gate_v, local_sem.at[2])
    gate_load.start()
    gu = Gather(
        me, up_ref, lambda who: up_v.at[pl.ds(who * rows_of, rows_of)],
        w_send.at[0], w_recv.at[0], local_sem.at[0],
    )
    gd = Gather(
        me, down_ref, lambda who: down_v.at[who], w_send.at[1], w_recv.at[1], local_sem.at[1]
    )
    barrier = pltpu.get_barrier_semaphore()
    for other in (gu.sib, gu.xn, gu.yn):
        pl.semaphore_signal(barrier, inc=1, device_id={"req": other}, device_id_type=MESH)

    @pl.when(z > 0)
    def _():
        pl.semaphore_signal(barrier, inc=1, device_id={"head": z - 1}, device_id_type=MESH)

    @pl.when(z < top)
    def _():
        pl.semaphore_signal(barrier, inc=1, device_id={"head": z + 1}, device_id_type=MESH)

    pl.semaphore_wait(
        barrier, 3 + (z > 0).astype(jnp.int32) + (z < top).astype(jnp.int32)
    )

    gu.begin()
    gd.begin()

    def line_copy(src, dst, send, recv, step):
        return pltpu.make_async_remote_copy(
            src_ref=src, dst_ref=dst, send_sem=send, recv_sem=recv,
            device_id={"head": z + step}, device_id_type=MESH,
        )

    class Sums:
        def __init__(self, phase, ups, dns, ups_out, dns_out):
            self.phase = phase
            self.bufs = {1: (ups_out, ups), -1: (dns_out, dns)}

        def copy(self, step, d, c):
            out, into = self.bufs[step]
            at = (self.phase, (1 - step) // 2, d, c)
            return line_copy(
                out.at[d, c], into.at[d, c], rs_send.at[at], rs_recv.at[at], step
            )

        def send(self, c):
            for k in range(heads - 1):
                for step, d in ((1, top - k), (-1, k)):
                    out, into = self.bufs[step]
                    goes = z < d if step == 1 else z > d
                    ends = z == 0 if step == 1 else z == top

                    @pl.when(jnp.logical_and(goes, ends))
                    def _():
                        out[d, c] = terms[d, c].astype(BF)
                        self.copy(step, d, c).start()

                    @pl.when(jnp.logical_and(goes, jnp.logical_not(ends)))
                    def _():
                        self.copy(step, d, c).wait_recv()
                        out[d, c] = (terms[d, c] + into[d, c].astype(F32)).astype(BF)
                        self.copy(step, d, c).start()

        def total(self, c, base):
            summed[c] = terms[z, c] + base
            for step in (1, -1):
                into = self.bufs[step][1]
                ends = z == 0 if step == 1 else z == top
                for d in range(heads):

                    @pl.when(jnp.logical_and(z == d, jnp.logical_not(ends)))
                    def _():
                        self.copy(step, d, c).wait_recv()
                        summed[c] = summed[c] + into[d, c].astype(F32)

        def finish(self):
            for step in (1, -1):
                for d in range(heads):

                    @pl.when(z < d if step == 1 else z > d)
                    def _():
                        for c in range(CHUNKS):
                            self.copy(step, d, c).wait_send()

    def ag_copy(step, hop, c):
        src = gath.at[z - step * (hop - 1), c]
        at = ((1 - step) // 2, hop - 1, c)
        return line_copy(src, src, ag_send.at[at], ag_recv.at[at], step)

    def ag_wait(step, hop, c):
        src = gath.at[z - step * hop, c]
        at = ((1 - step) // 2, hop - 1, c)
        line_copy(src, src, ag_send.at[at], ag_recv.at[at], -step).wait_recv()

    def sends(step, hop):
        if step == 1:
            return jnp.logical_and(z < top, z - (hop - 1) >= 0)
        return jnp.logical_and(z > 0, z + (hop - 1) <= top)

    def receives(step, hop):
        return z - hop >= 0 if step == 1 else z + hop <= top

    def ag_own(c):
        gath[z, c] = (summed[c] * gain_ref[z]).astype(BF)
        for step in (1, -1):

            @pl.when(sends(step, 1))
            def _():
                ag_copy(step, 1, c).start()

    def ag_forward(c):
        for hop in range(1, heads):
            for step in (1, -1):

                @pl.when(receives(step, hop))
                def _():
                    ag_wait(step, hop, c)

                if hop < heads - 1:

                    @pl.when(sends(step, hop + 1))
                    def _():
                        ag_copy(step, hop + 1, c).start()

    def ag_finish():
        for hop in range(1, heads):
            for step in (1, -1):

                @pl.when(sends(step, hop))
                def _():
                    for c in range(CHUNKS):
                        ag_copy(step, hop, c).wait_send()

    def base(c):
        return st_ref[pl.ds(c * rows, rows), :].astype(F32)

    def project(c):
        for b in range(projg_ref.shape[0]):
            terms[b // 2, c, :, pl.ds((b % 2) * 256, 256)] = mm(
                att_ref[pl.ds(c * rows, rows), :], projg_ref[b]
            )

    def feed(c):
        squares = jnp.zeros((rows, 1), F32)
        for o in range(heads):
            plain = gath[o, c].astype(F32) / gain_ref[o]
            squares = squares + jnp.sum(plain * plain, axis=1, keepdims=True)
        scale = lax.rsqrt(squares / width + norm_eps)

        def tile(t, carry):
            at = pl.ds(pl.multiple_of(t * 256, 256), 256)
            gate = jnp.zeros((rows, 256), F32)
            up = jnp.zeros((rows, 256), F32)
            for o in range(heads):
                u = gath[o, c]
                gate = gate + mm(u, gate_v[pl.ds(o * share, share), at])
                up = up + mm(u, up_v[pl.ds(o * share, share), at])
            gate = gate * scale
            hidden[:, at] = (gate / (1.0 + jnp.exp(-gate)) * (up * scale)).astype(BF)
            return carry

        lax.fori_loop(0, hidden.shape[1] // 256, tile, 0)
        for b in range(down_v.shape[0]):
            terms[b // 2, c, :, pl.ds((b % 2) * 256, 256)] = mm(hidden[...], down_v[b])

    one = Sums(0, up1, dn1, up1s, dn1s)
    two = Sums(1, up2, dn2, up2s, dn2s)
    project(0)
    one.send(0)
    project(1)
    one.send(1)
    project(2)
    one.total(0, base(0))
    ag_own(0)
    one.send(2)
    gu.middle()
    one.total(1, base(1))
    ag_own(1)
    ag_forward(0)
    one.total(2, base(2))
    ag_own(2)
    gd.middle()
    gu.last()
    ag_forward(1)
    ag_forward(2)
    gd.last()
    gate_load.wait()
    gu.finish()
    gd.finish()
    feed(0)
    two.send(0)
    feed(1)
    two.send(1)
    feed(2)
    two.total(0, summed[0])
    two.send(2)
    two.total(1, summed[1])
    two.total(2, summed[2])
    for c in range(CHUNKS):
        res_ref[pl.ds(c * rows, rows), :] = summed[c].astype(BF)
    one.finish()
    two.finish()
    ag_finish()


def padded(array, rows, fill=0):
    return jnp.pad(array, ((0, rows - array.shape[0]), (0, 0)), constant_values=fill)


def signed_tables(positions):
    cosine, sine = rope_tables(positions, HEAD_SIZE)
    half = HEAD_SIZE // 2
    return cosine, jnp.concatenate([-sine[:, :half], sine[:, half:]], axis=1)


def fast_body(
    prefill_query, prefill_new_pairs, prefill_cache, prefill_start, decode_query, decode_fresh,
    decode_cache, decode_length, decode_slot, prefill_states, decode_states, output_proj,
    norm_gain, gate_weight, up_weight, down_weight,
):
    n = lax.axis_size("req")
    heads = lax.axis_size("head")
    span, share = prefill_query.shape
    slots = decode_query.shape[0]
    rows = span + PAD
    cosine, sine = signed_tables(prefill_start[0] + jnp.arange(span, dtype=jnp.int32))
    dcos, dsin = signed_tables(jnp.pad(decode_length, (0, 8 - slots)))
    start = jnp.broadcast_to(prefill_start[:, None], (8, 128))
    lens = jnp.pad(decode_length, (0, 8 - slots), constant_values=1)
    dlen = jnp.broadcast_to(jnp.concatenate([lens, lens])[:, None], (16, 128))
    rid = (decode_slot // slots) * PAD + decode_slot % slots
    rid = jnp.broadcast_to(jnp.pad(rid, (0, PAD - slots), constant_values=-1)[:, None], (PAD, 128))
    marks = jnp.broadcast_to(
        jnp.pad(decode_slot, (0, PAD - slots), constant_values=-1)[:, None], (PAD, 128)
    ).astype(BF)
    token = jnp.concatenate(
        [padded(decode_query, PAD), padded(decode_fresh.reshape(slots, -1), PAD), marks], axis=1
    )
    vm = pl.BlockSpec(memory_space=pltpu.VMEM)
    hbm = pl.BlockSpec(memory_space=pl.ANY)
    dma = pltpu.SemaphoreType.DMA
    cache = prefill_cache.shape[2]
    kv = prefill_cache.shape[3]
    ff = gate_weight.shape[1]
    att, projg, gateg = pl.pallas_call(
        functools.partial(attention_kernel, n, slots),
        out_shape=[
            jax.ShapeDtypeStruct((rows, share), BF),
            jax.ShapeDtypeStruct((n,) + output_proj.shape, BF),
            jax.ShapeDtypeStruct((n * gate_weight.shape[0], ff), BF),
        ],
        in_specs=[vm, vm, vm, hbm, vm, vm, vm, vm, vm, vm, vm, vm, hbm, hbm, hbm],
        out_specs=[vm, hbm, hbm],
        scratch_shapes=[
            pltpu.VMEM((cache + span, kv), BF),
            pltpu.VMEM((cache + span, kv), BF),
            pltpu.VMEM(decode_cache.shape, BF),
            pltpu.VMEM((n, PAD, token.shape[1]), BF),
            pltpu.VMEM((n, PAD, share), BF),
            pltpu.VMEM((PAD, share), BF),
            pltpu.VMEM((span, share), BF),
            dma((5,)), dma((n,)), dma((n,)), dma((n,)), dma((n,)), dma((2, 9)), dma((2, 9)),
        ],
        compiler_params=pltpu.CompilerParams(
            collective_id=0, has_side_effects=True, vmem_limit_bytes=48 * 2**20
        ),
        cost_estimate=pl.CostEstimate(
            flops=3 * 10**9, bytes_accessed=30 * 10**6, transcendentals=6 * 10**6
        ),
        name="attend_and_gather",
    )(
        prefill_query, prefill_new_pairs[:, 0], prefill_new_pairs[:, 1], prefill_cache[0],
        cosine, sine, start, token, dcos, dsin, dlen, rid, decode_cache, output_proj, gate_weight,
    )
    states = jnp.concatenate([prefill_states, padded(decode_states, PAD)], axis=0)
    gain = norm_gain.astype(F32).reshape(heads, 1, share)
    line = (heads, CHUNKS, rows // CHUNKS, share)
    result = pl.pallas_call(
        functools.partial(layer_kernel, heads),
        out_shape=jax.ShapeDtypeStruct((rows, share), BF),
        in_specs=[vm, vm, vm, vm, hbm, hbm, hbm],
        out_specs=vm,
        scratch_shapes=[
            pltpu.VMEM(line, F32),
            pltpu.VMEM(line[1:], F32),
            pltpu.VMEM(line, BF),
            pltpu.VMEM((rows // CHUNKS, ff), BF),
            pltpu.VMEM(gateg.shape, BF),
            pltpu.VMEM(gateg.shape, BF),
            pltpu.VMEM((n,) + down_weight.shape, BF),
        ]
        + [pltpu.VMEM(line, BF)] * 8
        + [
            dma((3,)), dma((2, 9)), dma((2, 9)),
            dma((2, 2, heads, CHUNKS)), dma((2, 2, heads, CHUNKS)),
            dma((2, heads - 1, CHUNKS)), dma((2, heads - 1, CHUNKS)),
        ],
        compiler_params=pltpu.CompilerParams(
            collective_id=1, has_side_effects=True, vmem_limit_bytes=60 * 2**20
        ),
        cost_estimate=pl.CostEstimate(
            flops=11 * 10**9, bytes_accessed=40 * 10**6, transcendentals=10**6
        ),
        name="project_and_feed",
    )(att, states, projg, gain, gateg, up_weight, down_weight)
    return result[:span], result[span:span + slots]


def solution(mesh):
    in_specs = (
        P("req", "head"),
        P("req", None, "head"),
        P("req", None, None, "head"),
        P("req"),
        P("req", "head"),
        P("req", None, "head"),
        P("req", None, None, "head"),
        P("req"),
        P("req"),
        P("req", "head"),
        P("req", "head"),
        P("head", "req"),
        P(),
        P("req", "head"),
        P("req", "head"),
        P("head", "req"),
    )
    out_specs = (P("req", "head"), P("req", "head"))
    fits = mesh.shape["req"] == 8
    return jax.shard_map(
        fast_body if fits else body, mesh=mesh, in_specs=in_specs, out_specs=out_specs, check_vma=False)
```
